512 devices in a mesh: land: 8 (over x, z_hi), dp: 64 (over z_lo, y, core).
Axes of the slice: x: 4, y: 8, z: 8 (z_hi: 2, z_lo: 4; z = z_hi * 4 + z_lo), core: 2. Of those that a mesh axis runs over, the one named last changes fastest.
Arguments:
- embeddings: bfloat16 [32768, 1280], P(('dp', 'land')), may hold values from -6 to 6
- landmarks: bfloat16 [8192, 1280], P(('land', 'dp')), may hold values from -6 to 6
- factor: bfloat16 [8192, 1024], P(('land', 'dp')), may hold values from -6 to 6
- centroids: bfloat16 [4096, 1024], P('land'), may hold values from -6 to 6
- assignment: int32 [32768], P('dp'), may hold values from 0 to 4095, as said below
Outputs:
- distances: float32 [32768, 4096], P('dp', 'land')
- new_centroids: float32 [4096, 1024], P(('land', 'dp'))
The draws below stay inside these ranges and needn't reach their ends.
Inputs may be any that keep to these rules, and one draw needn't show every extreme that they name: `assignment`: among the 512 rows of one index of dp, at most 2 are assigned to centroids of any one aligned block of 8 centroid numbers.
All inputs are finite; a program needn't handle non-finite values.
Results may differ from the reference program's by a relative error of at most 0.01.
Values may be sent and summed in bfloat16 or wider, within the bound.
A program may use at most 64 MiB of HBM per device.

```python
import jax
import jax.numpy as jnp
from jax import lax

E = 1280
F = 1024
KC = 4096
ROWS = 512
LM_BLOCK = 1024
N_ROWS = 32768
LANDMARKS = 8192
OWN = 8
SLOTS = 2
N_LAND = 8
N_DP = 64


def centres_of(key):
    clusters = max(LANDMARKS // 32, 2)
    return jax.random.truncated_normal(jax.random.fold_in(key, 7), -4.0, 4.0, (clusters, E), jnp.float32)


def clustered(key, count, tag):
    centres = centres_of(key)
    own_key = jax.random.fold_in(key, tag)
    member = jax.random.randint(jax.random.fold_in(own_key, 1), (count,), 0, centres.shape[0])
    noise_part = jax.random.truncated_normal(jax.random.fold_in(own_key, 2), -4.0, 4.0, (count, E), jnp.float32)
    mix_weight = jax.random.uniform(jax.random.fold_in(own_key, 3), (count, 1), jnp.float32, 0.5, 0.95)
    points = mix_weight * centres[member] + jnp.sqrt(1.0 - mix_weight * mix_weight) * noise_part
    return jnp.clip(points, -6.0, 6.0)


def draw_embeddings(key, part):
    return clustered(key, N_ROWS, 11).astype(jnp.bfloat16)


def draw_landmarks(key, part):
    return clustered(key, LANDMARKS, 13).astype(jnp.bfloat16)


def draw_assignment(key, part):
    slices = N_LAND * N_DP
    seat_total = slices * SLOTS
    full_slice = jax.random.randint(jax.random.fold_in(key, 101), (), 0, slices)
    seat_ids = jnp.arange(seat_total, dtype=jnp.int32)

    def one_block(block_key):
        seat_order = jax.random.permutation(jax.random.fold_in(block_key, 1), seat_total).astype(jnp.int32)
        forced = seat_ids // SLOTS == full_slice
        scores = jnp.where(forced, -1 - seat_ids % SLOTS, seat_order)
        chosen = jnp.argsort(scores, stable=True)[:ROWS].astype(jnp.int32)
        shuffle = jax.random.permutation(jax.random.fold_in(block_key, 2), ROWS)
        chosen = chosen[shuffle]
        within = jax.random.randint(jax.random.fold_in(block_key, 3), (ROWS,), 0, OWN)
        return chosen // SLOTS * OWN + within
    block_keys = jax.random.split(jax.random.fold_in(key, 103), N_DP)
    return jax.vmap(one_block)(block_keys).reshape(N_ROWS).astype(jnp.int32)


def level_of(rng, shape, cuts, smallest, high):
    gain = 1.0
    for position, parts in cuts:
        draws = jax.random.uniform(jax.random.fold_in(jax.random.fold_in(rng, 6), position), (parts,), jnp.float32, smallest / len(cuts), high / len(cuts))
        gain = gain * jnp.repeat(jnp.exp(draws), shape[position] // parts).reshape((-1,) + (1,) * (len(shape) - 1 - position))
    return gain


def gaussian(stream_key, shape, scale, bound, cuts=(), kind=jnp.bfloat16):
    array = scale * jax.random.normal(stream_key, shape, jnp.float32)
    if cuts:
        array = array * level_of(stream_key, shape, cuts, -0.22, 0.18)
    return jnp.clip(array, -bound, bound).astype(kind)


def setup_inputs(seed: int = 0) -> dict:
    seeds = jax.random.split(jax.random.key(seed), 6)
    embeddings = draw_embeddings(jax.random.fold_in(seeds[5], 71), 0)
    landmarks = draw_landmarks(jax.random.fold_in(seeds[5], 71), 0)
    factor = gaussian(seeds[2], (LANDMARKS, F), 1.0, 6.0, ((0, 512),))
    centroids = gaussian(seeds[3], (KC, F), 1.0, 6.0, ((0, 8),))
    assignment = draw_assignment(jax.random.fold_in(seeds[5], 71), 0)
    return dict(embeddings=embeddings, landmarks=landmarks, factor=factor, centroids=centroids, assignment=assignment)


EPSILON = 1e-06
SHARPNESS = 6.0

def reference(embeddings, landmarks, factor, centroids, assignment):
    land_scale = lax.rsqrt(lax.optimization_barrier(jnp.mean(jnp.square(landmarks.astype(jnp.float32)), axis=1)) + EPSILON)
    cent_sq = lax.optimization_barrier(jnp.sum(jnp.square(centroids.astype(jnp.float32)), axis=1))
    factor_blocks = factor.reshape(N_LAND, LM_BLOCK, F).astype(jnp.float32)
    row_groups = embeddings.reshape(N_DP, ROWS, E)

    def one_group(group_rows):
        row_scale = lax.rsqrt(lax.optimization_barrier(jnp.mean(jnp.square(group_rows.astype(jnp.float32)), axis=1)) + EPSILON)
        inner_dots = jnp.dot(group_rows, landmarks.T, preferred_element_type=jnp.float32)
        similarity = inner_dots * row_scale[:, None] * land_scale[None, :] / E
        kernel = jnp.exp(SHARPNESS * (similarity - 1.0)).astype(jnp.bfloat16)
        kernel_wide = kernel.reshape(ROWS, N_LAND, LM_BLOCK).astype(jnp.float32)
        partial_value = jnp.einsum('rbm,bmf->brf', kernel_wide, factor_blocks).astype(jnp.bfloat16)
        features = lax.optimization_barrier(jnp.sum(partial_value.astype(jnp.float32), axis=0)).astype(jnp.bfloat16)
        feat_sq = lax.optimization_barrier(jnp.sum(jnp.square(features.astype(jnp.float32)), axis=1))
        cross_term = jnp.dot(features, centroids.T, preferred_element_type=jnp.float32)
        group_dist = (feat_sq[:, None] + cent_sq[None, :] - 2.0 * cross_term) / F
        return (group_dist, features)
    group_dist, all_features = lax.map(one_group, row_groups)
    distances = group_dist.reshape(N_ROWS, KC)
    all_features = all_features.reshape(N_ROWS, F).astype(jnp.float32)
    totals = jax.ops.segment_sum(all_features, assignment, num_segments=KC)
    counts = jax.ops.segment_sum(jnp.ones((N_ROWS,), jnp.float32), assignment, num_segments=KC)
    new_centroids = totals / jnp.maximum(counts, 1.0)[:, None]
    return (distances, new_centroids)
```

```python
import functools

import jax
import jax.numpy as jnp
from jax import lax
from jax.experimental import pallas as pl
from jax.experimental.pallas import tpu as pltpu
from jax.sharding import PartitionSpec as P

EPSILON = 1e-06
SHARPNESS = 6.0
MESH = pl.DeviceIdType.MESH
BF16 = jnp.bfloat16
F32 = jnp.float32

NX, NZ, NY = 4, 8, 8
EW = 1280
FW = 1024
Q = 4
QW = FW // Q
H = 2
HW = FW // H
N_SEM = 170

POS = {4: 0, 5: 1, 3: 2, 6: 3, 2: 4, 7: 5, 1: 6, 0: 7}


def kernel(
    e_ref, l_ref, f_ref, c_ref, a_ref,
    dist_ref, newc_ref,
    ebuf, lbuf, fbuf, kbuf, pbuf, rbuf, feat, abuf, obuf, arr, tsend, trecv, csend, crecv,
    rowc, markc, ss, rs,
):
    land = lax.axis_index("land")
    dp = lax.axis_index("dp")
    x, zh = land // 2, land % 2
    zl, y, c = dp // 16, (dp // 2) % 8, dp % 2
    z = zh * 4 + zl

    def device(dx=0, dz=0, dy=0, dc=0):
        xx, zz, yy, cc = (x + dx) % NX, (z + dz) % NZ, (y + dy) % NY, (c + dc) % 2
        return (xx * 2 + zz // 4, (zz % 4) * 16 + yy * 2 + cc)

    def near(rz, rc):
        return (land, ((zl + rz) % 4) * 16 + y * 2 + (c + rc) % 2)

    y_up, y_down = device(dy=1), device(dy=7)
    x_up, x_down = device(dx=1), device(dx=3)
    z_up, z_down = device(dz=1), device(dz=7)
    z_far = device(dz=4)
    sibling = device(dc=1)
    y_peer = {d: device(dy=d) for d in range(1, 8)}
    x_peer = {d: device(dx=d) for d in range(1, 4)}
    zc_peer = {i: near(i // 2, i % 2) for i in range(1, 8)}

    barrier = pltpu.get_barrier_semaphore()
    peers = [*y_peer.values(), *x_peer.values(), z_up, z_down, z_far, *zc_peer.values()]
    for peer in peers:
        pl.semaphore_signal(barrier, inc=1, device_id=peer, device_id_type=MESH)
    pl.semaphore_wait(barrier, len(peers))

    copies = []

    def send(src, dst, peer):
        k = len(copies)
        copy = pltpu.make_async_remote_copy(
            src_ref=src, dst_ref=dst, send_sem=ss.at[k], recv_sem=rs.at[k],
            device_id=peer, device_id_type=MESH,
        )
        copy.start()
        copies.append(copy)
        return copy

    def got(*arrived):
        for copy in arrived:
            copy.wait_recv()

    def send_e(k):
        up = e_ref if k == 1 else ebuf.at[POS[k - 1]]
        down = e_ref if k == 1 else ebuf.at[POS[9 - k]]
        if k < 4:
            return (
                send(up, ebuf.at[POS[k]], y_up),
                send(down, ebuf.at[POS[8 - k]], y_down),
            )
        return (
            send(up.at[pl.ds(0, 32)], ebuf.at[POS[4], pl.ds(0, 32)], y_up),
            send(down.at[pl.ds(32, 32)], ebuf.at[POS[4], pl.ds(32, 32)], y_down),
        )

    def send_lz(k):
        up = l_ref if k == 1 else lbuf.at[0, 0, k - 1]
        down = l_ref if k == 1 else lbuf.at[0, 0, 9 - k]
        if k < 4:
            return (
                send(up, lbuf.at[0, 0, k], z_up),
                send(down, lbuf.at[0, 0, 8 - k], z_down),
            )
        first, second = pl.ds(0, EW // 2), pl.ds(EW // 2, EW // 2)
        return (
            send(up.at[:, first], lbuf.at[0, 0, 4, :, first], z_up),
            send(down.at[:, second], lbuf.at[0, 0, 4, :, second], z_down),
        )

    def send_lx(dz):
        src = l_ref if dz == 0 else lbuf.at[0, 0, dz]
        return (
            send(src, lbuf.at[1, 0, dz], x_up),
            send(src, lbuf.at[3, 0, dz], x_down),
        )

    def send_lx2(dz):
        if dz < 4:
            return send(lbuf.at[1, 0, dz], lbuf.at[2, 0, dz], x_up)
        return send(lbuf.at[3, 0, dz], lbuf.at[2, 0, dz], x_down)

    def send_fz(k):
        up, down = fbuf.at[:, 0, k - 1], fbuf.at[:, 0, (9 - k) % 8]
        if k < 4:
            return (
                send(up, fbuf.at[:, 0, k], z_up),
                send(down, fbuf.at[:, 0, 8 - k], z_down),
            )
        first, second = pl.ds(0, 2), pl.ds(2, 2)
        return (
            send(fbuf.at[first, 0, 3], fbuf.at[first, 0, 4], z_up),
            send(fbuf.at[second, 0, 5], fbuf.at[second, 0, 4], z_down),
        )

    def send_fs(k):
        return send(fbuf.at[:, 0, k], fbuf.at[:, 1, k], sibling)

    def send_ls(dx):
        return send(lbuf.at[dx, 0], lbuf.at[dx, 1], sibling)

    fx1 = (send(f_ref, fbuf.at[1, 0, 0], x_up), send(f_ref, fbuf.at[3, 0, 0], x_down))
    lz = {1: send_lz(1)}
    e = {1: send_e(1)}
    lx = {0: send_lx(0)}
    ids_in = [send(a_ref, abuf.at[d], y_peer[d]) for d in range(1, 8)]
    ebuf[POS[0]] = e_ref[...]
    lbuf[0, 0, 0] = l_ref[...]
    fbuf[0, 0, 0] = f_ref[...]
    abuf[0] = a_ref[...]

    def targets(a):
        block = a >> 3
        to = block & 63
        ry = ((to >> 1) - y) & 7
        rz = ((to >> 4) - zl) & 3
        rc = (to - c) & 1
        at = ry * 8 + rz * 2 + rc
        return jnp.where((block >> 6) == land, at, -1), (a & 7).astype(F32)

    def picks(at, base, count):
        shape = (count, at.shape[1])
        here = jnp.broadcast_to(at, shape) == lax.broadcasted_iota(jnp.int32, shape, 0) + base
        row = lax.broadcasted_iota(jnp.int32, shape, 1).astype(F32)
        first = jnp.min(jnp.where(here, row, 1e4), axis=1, keepdims=True)
        last = jnp.max(jnp.where(here, row, -1.0), axis=1, keepdims=True)
        one = jnp.where(here & (row == first), 1.0, 0.0)
        two = jnp.where(here & (row == last) & (last != first), 1.0, 0.0)
        return one, two

    def across(column):
        n = column.shape[0]
        spread = jnp.broadcast_to(column, (n, n))
        eye = lax.broadcasted_iota(jnp.int32, (n, n), 0) == lax.broadcasted_iota(jnp.int32, (n, n), 1)
        return jnp.sum(jnp.where(eye, spread, 0.0), axis=0, keepdims=True)

    at, _ = targets(a_ref[...])
    one, two = picks(at, 0, 64)
    pick = jnp.concatenate([one.reshape(8, 8, 512), two.reshape(8, 8, 512)], axis=1)
    pick = pick.reshape(128, 512).astype(BF16)

    got(*fx1)
    half_a, half_b = pl.ds(0, FW // 2), pl.ds(FW // 2, FW // 2)
    fx2 = (
        send(fbuf.at[1, 0, 0, :, half_a], fbuf.at[2, 0, 0, :, half_a], x_up),
        send(fbuf.at[3, 0, 0, :, half_b], fbuf.at[2, 0, 0, :, half_b], x_down),
    )
    got(*lz[1])
    lz[2] = send_lz(2)
    lx[1], lx[7] = send_lx(1), send_lx(7)
    got(*fx2)
    fz = {1: send_fz(1)}
    fs = {0: send_fs(0)}
    got(*lz[2])
    lz[3] = send_lz(3)
    lx[2], lx[6] = send_lx(2), send_lx(6)
    got(*e[1])
    e[2] = send_e(2)

    got(*ids_in)
    ids = []
    for d in range(8):
        at, local_id = targets(abuf[d])
        near_at = jnp.where((at >= 0) & ((((abuf[d] >> 4) & 7) - y) & 7 == 0), at & 7, -1)
        for chosen in picks(near_at, 0, 8):
            ids.append(jnp.sum(chosen * (local_id + 1.0), axis=1, keepdims=True) - 1.0)
    ids = across(jnp.concatenate(ids, axis=0))
    row = lax.broadcasted_iota(jnp.int32, (64, 128), 0)
    column = lax.broadcasted_iota(jnp.int32, (64, 128), 1)
    match = ((row >> 3) == (column & 7)) & ((row & 7).astype(F32) == jnp.broadcast_to(ids, (64, 128)))
    match = jnp.where(match, 1.0, 0.0)
    csend[...] = jnp.broadcast_to(jnp.sum(match, axis=1, keepdims=True), (64, 128)).reshape(8, 8, 128)
    match = match.astype(BF16)
    counts_in = [send(csend.at[i], crecv.at[i], zc_peer[i]) for i in range(1, 8)]

    lx2 = {}
    got(*lx[0])
    lx2[0] = send_lx2(0)
    got(*fz[1])
    fz[2] = send_fz(2)
    fs[1], fs[7] = send_fs(1), send_fs(7)
    got(*lz[3])
    lz[4] = send_lz(4)
    lx[3], lx[5] = send_lx(3), send_lx(5)
    got(*lx[1], *lx[7])
    lx2[1], lx2[7] = send_lx2(1), send_lx2(7)
    got(*e[2])
    e[3] = send_e(3)
    got(*fz[2])
    fz[3] = send_fz(3)
    fs[2], fs[6] = send_fs(2), send_fs(6)
    got(*lz[4])
    lx[4] = send_lx(4)
    ls = {0: send_ls(0)}
    got(*lx[2], *lx[6])
    lx2[2], lx2[6] = send_lx2(2), send_lx2(6)

    cents = c_ref[...]
    cent_sq = jnp.sum(jnp.square(cents.astype(F32)), axis=1, keepdims=True)
    cent_sq = jnp.concatenate([across(cent_sq[k * 128 : (k + 1) * 128]) for k in range(4)], axis=1)

    got(*fz[3])
    fz[4] = send_fz(4)
    fs[3], fs[5] = send_fs(3), send_fs(5)
    got(*lx[3], *lx[5], *lx[4])
    lx2[3], lx2[5], lx2[4] = send_lx2(3), send_lx2(5), send_lx2(4)
    ls[1], ls[3] = send_ls(1), send_ls(3)
    got(*e[3])
    e[4] = send_e(4)

    def row_coef(g):
        rows = ebuf[2 * g : 2 * g + 2].reshape(128, EW).astype(F32)
        mean = jnp.sum(rows * rows, axis=1, keepdims=True) * (1.0 / EW)
        rowc[g * 128 : (g + 1) * 128, :] = lax.rsqrt(mean + EPSILON) * (SHARPNESS / EW)

    def mark_coef(dx):
        marks = lbuf[dx].reshape(256, EW).astype(F32)
        mean = jnp.sum(marks * marks, axis=1, keepdims=True) * (1.0 / EW)
        scale = lax.rsqrt(mean + EPSILON)
        markc[dx] = jnp.concatenate([across(scale[:128]), across(scale[128:])], axis=1)

    def similar(g, dx):
        dots = lax.dot_general(
            ebuf[2 * g : 2 * g + 2].reshape(128, EW), lbuf[dx].reshape(256, EW),
            (((1,), (1,)), ((), ())), preferred_element_type=F32,
        )
        rows = slice(g * 128, (g + 1) * 128)
        value = jnp.exp(dots * rowc[rows, :] * markc[dx] - SHARPNESS)
        kbuf[rows, dx * 256 : (dx + 1) * 256] = value.astype(BF16)

    row_coef(3)
    row_coef(2)
    row_coef(1)
    got(ls[0])
    mark_coef(0)
    for g in (3, 2, 1):
        similar(g, 0)
    got(*fz[4])
    fs[4] = send_fs(4)
    got(ls[1], ls[3])
    for dx in (1, 3):
        mark_coef(dx)
        for g in (3, 2, 1):
            similar(g, dx)
    got(*lx2.values())
    ls[2] = send_ls(2)
    got(*e[4])
    row_coef(0)
    for dx in (0, 1, 3):
        similar(0, dx)
    got(ls[2])
    mark_coef(2)
    for g in range(4):
        similar(g, 2)
    got(*fs.values())

    def partial(g):
        for q in range(Q):
            cols = slice(q * QW, (q + 1) * QW)
            value = jnp.dot(
                kbuf[g * 128 : (g + 1) * 128, :], fbuf[:, :, :, :, cols].reshape(1024, QW),
                preferred_element_type=F32,
            )
            pbuf[2 * g : 2 * g + 2, :, cols] = value.reshape(2, 64, QW).astype(BF16)

    def length(q, way):
        return 4 if (q + way) % 2 == 0 else 3

    def slot(q, way, t):
        left = length(q, way) - t
        return POS[left if way == 0 else (8 - left) % 8]

    toward = (y_down, y_up)

    def part(q):
        return pl.ds(q * QW, QW)

    chain = {}

    def begin(q, way):
        chain[q, way] = send(pbuf.at[slot(q, way, 0), :, part(q)], rbuf.at[q, way, 0], toward[way])

    partial(0)
    for q in range(Q):
        begin(q, 0 if q % 2 == 0 else 1)
        if q % 2 == 0:
            begin(q, 1)
    partial(1)
    for q in range(Q):
        if q % 2 == 1:
            begin(q, 0)
    partial(2)
    partial(3)

    def finish(q):
        cols = slice(q * QW, (q + 1) * QW)
        total = pbuf[POS[0], :, cols].astype(F32)
        for way in range(2):
            total += rbuf[q, way, length(q, way) - 1].astype(F32)
        feat[land, :, cols] = total.astype(BF16)
        own = feat.at[land, :, part(q)]
        return send(own, own, z_far), [send(own, own, x_peer[d]) for d in (1, 3, 2)]

    def relay(q):
        other = feat.at[land + 1 - 2 * zh, :, part(q)]
        return [send(other, other, x_peer[d]) for d in (1, 3, 2)]

    gather = {}
    for t in range(1, 5):
        for q in range(Q):
            for way in range(2):
                n = length(q, way)
                if t > n:
                    continue
                got(chain[q, way])
                if t < n:
                    cols = slice(q * QW, (q + 1) * QW)
                    rbuf[q, way, t - 1] = (
                        rbuf[q, way, t - 1].astype(F32) + pbuf[slot(q, way, t), :, cols].astype(F32)
                    ).astype(BF16)
                    chain[q, way] = send(rbuf.at[q, way, t - 1], rbuf.at[q, way, t], toward[way])
            if t == 4:
                gather[q] = finish(q)
    arriving = []
    for q in range(Q):
        far, around = gather[q]
        got(far)
        arriving.append(around + relay(q))

    step1 = {}
    for h in range(H):
        for q in range(h * Q // H, (h + 1) * Q // H):
            got(*arriving[q])
        cols = slice(h * HW, (h + 1) * HW)
        chosen = jnp.dot(pick, feat[:, :, cols].reshape(512, HW), preferred_element_type=F32)
        obuf[:, :, cols] = chosen.reshape(8, 16, HW).astype(BF16)
        arr[0, :, cols] = chosen[:16].astype(BF16)
        ds = pl.ds(h * HW, HW)
        step1[h] = [send(obuf.at[d, :, ds], arr.at[d, :, ds], y_peer[d]) for d in range(1, 8)]

    for b in range(4):
        rows = feat[2 * b : 2 * b + 2].reshape(128, FW)
        wide = rows.astype(F32)
        feat_sq = jnp.sum(wide * wide, axis=1, keepdims=True)
        cross = lax.dot_general(rows, c_ref[...], (((1,), (1,)), ((), ())), preferred_element_type=F32)
        dist_ref[b * 128 : (b + 1) * 128, :] = (feat_sq + cent_sq - 2.0 * cross) * (1.0 / FW)

    step2 = {}
    mine = []
    for h in range(H):
        got(*step1[h])
        cols = slice(h * HW, (h + 1) * HW)
        sums = jnp.dot(match, arr[:, :, cols].reshape(128, HW), preferred_element_type=F32)
        mine.append(sums[:8])
        sums = sums.reshape(8, 8, HW)
        tsend[h] = jnp.concatenate([sums[:, :, : HW // 2], sums[:, :, HW // 2 :]], axis=1).astype(BF16)
        step2[h] = [send(tsend.at[h, i], trecv.at[h, i], zc_peer[i]) for i in range(1, 8)]

    got(*counts_in)
    counts = csend[0]
    for i in range(1, 8):
        counts += crecv[i]
    scale = 1.0 / jnp.maximum(counts[:, :1], 1.0)
    for h in range(H):
        got(*step2[h])
        total = jnp.sum(trecv[h, 1:].astype(F32), axis=0)
        total = mine[h] + jnp.concatenate([total[:8], total[8:]], axis=1)
        newc_ref[:, h * HW : (h + 1) * HW] = total * scale

    for copy in copies:
        copy.wait_send()


def local(embeddings, landmarks, factor, centroids, assignment):
    vmem = pl.BlockSpec(memory_space=pltpu.VMEM)
    return pl.pallas_call(
        kernel,
        out_shape=(
            jax.ShapeDtypeStruct((512, 512), F32),
            jax.ShapeDtypeStruct((8, FW), F32),
        ),
        in_specs=[vmem] * 5,
        out_specs=(vmem, vmem),
        scratch_shapes=[
            pltpu.VMEM((8, 64, EW), BF16),
            pltpu.VMEM((4, 2, 8, 16, EW), BF16),
            pltpu.VMEM((4, 2, 8, 16, FW), BF16),
            pltpu.VMEM((512, 1024), BF16),
            pltpu.VMEM((8, 64, FW), BF16),
            pltpu.VMEM((Q, 2, 4, 64, QW), BF16),
            pltpu.VMEM((8, 64, FW), BF16),
            pltpu.VMEM((8, 1, 512), jnp.int32),
            pltpu.VMEM((8, 16, FW), BF16),
            pltpu.VMEM((8, 16, FW), BF16),
            pltpu.VMEM((H, 8, 16, HW // 2), BF16),
            pltpu.VMEM((H, 8, 16, HW // 2), BF16),
            pltpu.VMEM((8, 8, 128), F32),
            pltpu.VMEM((8, 8, 128), F32),
            pltpu.VMEM((512, 1), F32),
            pltpu.VMEM((4, 1, 256), F32),
            pltpu.SemaphoreType.DMA((N_SEM,)),
            pltpu.SemaphoreType.DMA((N_SEM,)),
        ],
        compiler_params=pltpu.CompilerParams(
            collective_id=0, has_side_effects=True, vmem_limit_bytes=48 << 20
        ),
        name="nystrom",
    )(embeddings, landmarks, factor, centroids, assignment.reshape(1, 512))


def solution(mesh):
    return jax.shard_map(
        local,
        mesh=mesh,
        in_specs=(
            P(("dp", "land"), None),
            P(("land", "dp"), None),
            P(("land", "dp"), None),
            P("land", None),
            P("dp"),
        ),
        out_specs=(P("dp", "land"), P(("land", "dp"), None)),
        check_vma=False,
    )
```

```python
import jax
import jax.numpy as jnp
from jax import lax
from jax.experimental import pallas as pl
from jax.experimental.pallas import tpu as pltpu
from jax.sharding import PartitionSpec as P

EPSILON = 1e-06
SHARPNESS = 6.0
MESH = pl.DeviceIdType.MESH
BF16 = jnp.bfloat16
F32 = jnp.float32

NX, NZ, NY = 4, 8, 8
EW = 1280
FW = 1024
Q = 4
QW = FW // Q
H = 2
HW = FW // H
N_SEM = 200

POS = {4: 0, 5: 1, 3: 2, 6: 3, 2: 4, 7: 5, 1: 6, 0: 7}

PER_KB = 0.02
PER_KB_SIBLING = 0.002
HOP = 1.4
STEP = 0.05


class Node:
    def __init__(self, needs, work=None, cost=0.0, rank=0.0, copy=None, links=(), hops=1, kb=0.0):
        self.needs, self.work, self.cost, self.rank = needs, work, cost, rank
        self.copy, self.links, self.hops, self.kb = copy, links, hops, kb


def emit(nodes, flying):
    clock, free, done = 0.0, {}, set()
    flying = [(HOP, k, node) for k, node in enumerate(flying)]
    waiting = list(nodes)
    count = len(flying)
    while waiting or flying:
        ready = [n for n in waiting if all(id(d) in done for d in n.needs)]
        sends = [n for n in ready if n.copy is not None]
        if sends:
            node = min(sends, key=lambda n: n.rank)
            node.copy.start()
            end = clock
            for link, hops in node.links:
                rate = PER_KB_SIBLING if link == "c" else PER_KB
                free[link] = max(clock, free.get(link, 0.0)) + node.kb * rate * hops
                end = max(end, free[link])
            flying.append((end + HOP + 0.4 * (node.hops - 1), count, node))
            count += 1
            clock += STEP
            waiting.remove(node)
            continue
        tasks = [n for n in ready if n.copy is None]
        soonest = min(flying) if flying else None
        if soonest and (soonest[0] <= clock or not tasks):
            flying.remove(soonest)
            (soonest[2].copy.wait_recv if soonest[2].links else soonest[2].copy.wait)()
            clock = max(clock, soonest[0]) + STEP
            done.add(id(soonest[2]))
            continue
        node = min(tasks, key=lambda n: n.rank)
        node.work()
        clock += node.cost
        done.add(id(node))
        waiting.remove(node)


def across(column):
    n = column.shape[0]
    spread = jnp.broadcast_to(column, (n, n))
    eye = lax.broadcasted_iota(jnp.int32, (n, n), 0) == lax.broadcasted_iota(jnp.int32, (n, n), 1)
    return jnp.sum(jnp.where(eye, spread, 0.0), axis=0, keepdims=True)


def kernel(
    e_ref, l_ref, f_ref, c_ref, a_ref,
    dist_ref, newc_ref,
    ebuf, lbuf, fbuf, cbuf, kbuf, pbuf, rbuf, feat, abuf, obuf, arr, tsend, trecv, csend, crecv,
    rowc, markc, centq, pickb, matchb, mine, ss, rs, ls,
):
    land = lax.axis_index("land")
    dp = lax.axis_index("dp")
    x, zh = land // 2, land % 2
    zl, y, c = dp // 16, (dp // 2) % 8, dp % 2
    z = zh * 4 + zl

    def device(dx=0, dz=0, dy=0, dc=0):
        xx, zz, yy, cc = (x + dx) % NX, (z + dz) % NZ, (y + dy) % NY, (c + dc) % 2
        return (xx * 2 + zz // 4, (zz % 4) * 16 + yy * 2 + cc)

    def near(rz, rc):
        return (land, ((zl + rz) % 4) * 16 + y * 2 + (c + rc) % 2)

    y_up, y_down = device(dy=1), device(dy=7)
    x_up, x_down = device(dx=1), device(dx=3)
    z_up, z_down = device(dz=1), device(dz=7)
    z_far = device(dz=4)
    sibling = device(dc=1)
    y_peer = {d: device(dy=d) for d in range(1, 8)}
    x_peer = {d: device(dx=d) for d in range(1, 4)}
    zc_peer = {i: near(i // 2, i % 2) for i in range(1, 8)}

    loads = []
    for src, dst in (
        (l_ref, lbuf.at[0, 0, 0]), (f_ref, fbuf.at[0, 0, 0]), (e_ref, ebuf.at[POS[0]]),
        (a_ref, abuf.at[0]), (c_ref, cbuf),
    ):
        copy = pltpu.make_async_copy(src, dst, ls.at[len(loads)])
        copy.start()
        loads.append(Node([], copy=copy))
    got_l, got_f, got_e, got_a, got_c = loads

    barrier = pltpu.get_barrier_semaphore()
    peers = [*y_peer.values(), *x_peer.values(), z_up, z_down, z_far, *zc_peer.values()]
    for peer in peers:
        pl.semaphore_signal(barrier, inc=1, device_id=peer, device_id_type=MESH)
    pl.semaphore_wait(barrier, len(peers))

    nodes = []
    copies = []

    def task(work, cost, needs, rank=0.0):
        nodes.append(Node(needs, work=work, cost=cost, rank=rank))
        return nodes[-1]

    def send(src, dst, peer, links, kb, needs, hops=1, rank=0.0):
        k = len(copies)
        copies.append(
            pltpu.make_async_remote_copy(
                src_ref=src, dst_ref=dst, send_sem=ss.at[k], recv_sem=rs.at[k],
                device_id=peer, device_id_type=MESH,
            )
        )
        nodes.append(Node(needs, copy=copies[k], links=links, kb=kb, hops=hops, rank=rank))
        return nodes[-1]

    YU, YD, XU, XD, ZU, ZD, SC = [((name, 1),) for name in ("y+", "y-", "x+", "x-", "z+", "z-", "c")]

    def far_y(d):
        return (("y+", d),) if d < 4 else (("y-", 8 - d),) if d > 4 else (("y+", 2), ("y-", 2))

    def far_x(d):
        return {1: XU, 3: XD, 2: (("x+", 1), ("x-", 1))}[d]

    fx = {0: got_f}
    fx[1] = send(fbuf.at[0, 0, 0], fbuf.at[1, 0, 0], x_up, XU, 32, [got_f])
    fx[3] = send(fbuf.at[0, 0, 0], fbuf.at[3, 0, 0], x_down, XD, 32, [got_f])
    half_a, half_b = pl.ds(0, FW // 2), pl.ds(FW // 2, FW // 2)
    fx2 = [
        send(fbuf.at[1, 0, 0, :, half_a], fbuf.at[2, 0, 0, :, half_a], x_up, XU, 16, [fx[1]]),
        send(fbuf.at[3, 0, 0, :, half_b], fbuf.at[2, 0, 0, :, half_b], x_down, XD, 16, [fx[3]]),
    ]

    lz = {0: [got_l]}
    for k in range(1, 4):
        lz[k] = [send(lbuf.at[0, 0, k - 1], lbuf.at[0, 0, k], z_up, ZU, 40, lz[k - 1])]
        lz[8 - k] = [send(lbuf.at[0, 0, (9 - k) % 8], lbuf.at[0, 0, 8 - k], z_down, ZD, 40, lz[(9 - k) % 8])]
    first, second = pl.ds(0, EW // 2), pl.ds(EW // 2, EW // 2)
    lz[4] = [
        send(lbuf.at[0, 0, 3, :, first], lbuf.at[0, 0, 4, :, first], z_up, ZU, 20, lz[3]),
        send(lbuf.at[0, 0, 5, :, second], lbuf.at[0, 0, 4, :, second], z_down, ZD, 20, lz[5]),
    ]

    half = [pl.ds(0, 32), pl.ds(32, 32)]
    e = {(0, 0): [got_e], (0, 1): [got_e]}
    for k in range(1, 5):
        for p in range(2):
            up, down = (k - 1, p), ((9 - k) % 8, p)
            if k < 4 or p == 0:
                e[k, p] = [send(ebuf.at[POS[up[0]], half[p]], ebuf.at[POS[k], half[p]], y_up, YU, 80, e[up])]
            if k < 4 or p == 1:
                e[8 - k, p] = [send(ebuf.at[POS[down[0]], half[p]], ebuf.at[POS[8 - k], half[p]], y_down, YD, 80, e[down])]

    lx = {}
    for dz in (0, 1, 7, 2, 6, 3, 5, 4):
        lx[0, dz] = lz[dz]
        lx[1, dz] = [send(lbuf.at[0, 0, dz], lbuf.at[1, 0, dz], x_up, XU, 40, lz[dz])]
        lx[3, dz] = [send(lbuf.at[0, 0, dz], lbuf.at[3, 0, dz], x_down, XD, 40, lz[dz])]
    for dz in (0, 1, 7, 2, 6, 3, 5, 4):
        if dz < 4:
            lx[2, dz] = [send(lbuf.at[1, 0, dz], lbuf.at[2, 0, dz], x_up, XU, 40, lx[1, dz])]
        else:
            lx[2, dz] = [send(lbuf.at[3, 0, dz], lbuf.at[2, 0, dz], x_down, XD, 40, lx[3, dz])]

    fz = {(0, 0): [got_f], (1, 0): [fx[1]], (3, 0): [fx[3]], (2, 0): fx2}
    for k in range(1, 4):
        for dx in (0, 1, 3, 2):
            up, down = (dx, k - 1), (dx, (9 - k) % 8)
            fz[dx, k] = [send(fbuf.at[dx, 0, up[1]], fbuf.at[dx, 0, k], z_up, ZU, 32, fz[up], rank=0.1)]
            fz[dx, 8 - k] = [send(fbuf.at[dx, 0, down[1]], fbuf.at[dx, 0, 8 - k], z_down, ZD, 32, fz[down], rank=0.1)]
    for dx in (0, 1):
        fz[dx, 4] = [send(fbuf.at[dx, 0, 3], fbuf.at[dx, 0, 4], z_up, ZU, 32, fz[dx, 3], rank=0.1)]
    for dx in (3, 2):
        fz[dx, 4] = [send(fbuf.at[dx, 0, 5], fbuf.at[dx, 0, 4], z_down, ZD, 32, fz[dx, 5], rank=0.1)]

    lsib = {}
    for dx in range(4):
        lsib[dx] = [
            send(
                lbuf.at[dx, 0, pl.ds(4 * p, 4)], lbuf.at[dx, 1, pl.ds(4 * p, 4)], sibling, SC, 160,
                [n for dz in range(4 * p, 4 * p + 4) for n in lx[dx, dz]],
            )
            for p in range(2)
        ]
    fsib = [
        send(fbuf.at[:, 0, k], fbuf.at[:, 1, k], sibling, SC, 128, [n for dx in range(4) for n in fz[dx, k]])
        for k in range(8)
    ]

    def targets(a):
        to = (a >> 3) & 63
        ry, rz, rc = ((to >> 1) - y) & 7, ((to >> 4) - zl) & 3, (to - c) & 1
        return (a >> 9) == land, ry, rz * 2 + rc

    def picks(at, at_row):
        row = lax.broadcasted_iota(jnp.int32, at.shape, 1).astype(F32)
        here = at == at_row
        first = jnp.min(jnp.where(here, row, 1e4), axis=1, keepdims=True)
        last = jnp.max(jnp.where(here, row, -1.0), axis=1, keepdims=True)
        one = jnp.where(here & (row == first), 1.0, 0.0)
        two = jnp.where(here & (row == last) & (last != first), 1.0, 0.0)
        return one, two

    def choose():
        inside, ry, rzc = targets(abuf[0])
        at = jnp.broadcast_to(jnp.where(inside, ry * 8 + rzc, -1), (64, 512))
        one, two = picks(at, lax.broadcasted_iota(jnp.int32, (64, 512), 0))
        both = jnp.concatenate([one.reshape(8, 8, 512), two.reshape(8, 8, 512)], axis=1)
        pickb[...] = both.reshape(128, 512).astype(BF16)

    chosen = task(choose, 1.0, [got_a], rank=1.0)

    ids_in = [send(abuf.at[0], abuf.at[d], y_peer[d], far_y(d), 2, [got_a], rank=0.05) for d in range(1, 8)]

    def matching():
        a = abuf[...]
        inside, ry, rzc = targets(a)
        at = jnp.broadcast_to(jnp.where(inside & (ry == 0), rzc, -1), (8, 8, 512)).reshape(64, 512)
        number = jnp.broadcast_to((a & 7).astype(F32) + 1.0, (8, 8, 512)).reshape(64, 512)
        ids = [
            jnp.sum(which * number, axis=1, keepdims=True).reshape(8, 8, 1)
            for which in picks(at, lax.broadcasted_iota(jnp.int32, (64, 512), 0) & 7)
        ]
        ids = across(jnp.concatenate(ids, axis=1).reshape(128, 1)) - 1.0
        row = lax.broadcasted_iota(jnp.int32, (64, 128), 0)
        column = lax.broadcasted_iota(jnp.int32, (64, 128), 1)
        match = ((row >> 3) == (column & 7)) & ((row & 7).astype(F32) == jnp.broadcast_to(ids, (64, 128)))
        match = jnp.where(match, 1.0, 0.0)
        csend[...] = jnp.broadcast_to(jnp.sum(match, axis=1, keepdims=True), (64, 128)).reshape(8, 8, 128)
        matchb[...] = match.astype(BF16)

    matched = task(matching, 1.2, [got_a, *ids_in], rank=8.0)
    counts_in = [send(csend.at[i], crecv.at[i], zc_peer[i], SC, 4, [matched], rank=0.2) for i in range(1, 8)]

    def square_centroids(k):
        def work():
            rows = cbuf[k * 128 : (k + 1) * 128, :].astype(F32)
            centq[:, k * 128 : (k + 1) * 128] = across(jnp.sum(rows * rows, axis=1, keepdims=True))
        return task(work, 0.4, [got_c], rank=9.0)

    squared = [square_centroids(k) for k in range(4)]

    places = {pos: j for j, pos in POS.items()}

    def e_group(g):
        return [n for j in (places[2 * g], places[2 * g + 1]) for p in range(2) for n in e[j, p]]

    def l_group(dx):
        return lsib[dx] + [n for dz in range(8) for n in lx[dx, dz]]

    def row_coef(g):
        def work():
            rows = ebuf[2 * g : 2 * g + 2].reshape(128, EW).astype(F32)
            mean = jnp.sum(rows * rows, axis=1, keepdims=True) * (1.0 / EW)
            rowc[g * 128 : (g + 1) * 128, :] = lax.rsqrt(mean + EPSILON) * (SHARPNESS / EW)
        return task(work, 0.3, e_group(g), rank=2.0)

    def mark_coef(dx):
        def work():
            marks = lbuf[dx].reshape(256, EW).astype(F32)
            mean = jnp.sum(marks * marks, axis=1, keepdims=True) * (1.0 / EW)
            scale = lax.rsqrt(mean + EPSILON)
            markc[dx] = jnp.concatenate([across(scale[:128]), across(scale[128:])], axis=1)
        return task(work, 0.5, l_group(dx), rank=2.0)

    row_done = [row_coef(g) for g in range(4)]
    mark_done = [mark_coef(dx) for dx in range(4)]

    def similar(g, dx):
        def work():
            dots = lax.dot_general(
                ebuf[2 * g : 2 * g + 2].reshape(128, EW), lbuf[dx].reshape(256, EW),
                (((1,), (1,)), ((), ())), preferred_element_type=F32,
            )
            rows = slice(g * 128, (g + 1) * 128)
            value = jnp.exp(dots * rowc[rows, :] * markc[dx] - SHARPNESS)
            kbuf[rows, dx * 256 : (dx + 1) * 256] = value.astype(BF16)
        return task(work, 0.35, [row_done[g], mark_done[dx]], rank=3.0 + 0.1 * g)

    tiles = {(g, dx): similar(g, dx) for g in range(4) for dx in range(4)}

    factor_in = [*fsib, *(n for pieces in fz.values() for n in pieces)]

    def partial(g, q):
        def work():
            cols = slice(q * QW, (q + 1) * QW)
            value = jnp.dot(
                kbuf[g * 128 : (g + 1) * 128, :], fbuf[:, :, :, :, cols].reshape(1024, QW),
                preferred_element_type=F32,
            )
            pbuf[2 * g : 2 * g + 2, :, cols] = value.reshape(2, 64, QW).astype(BF16)
        return task(work, 0.25, [*factor_in, *(tiles[g, dx] for dx in range(4))], rank=4.0 + g)

    parts = {(g, q): partial(g, q) for g in range(4) for q in range(Q)}

    def part(q):
        return pl.ds(q * QW, QW)

    def chain(q, way):
        steps = 4 if (q + way) % 2 == 0 else 3
        peer, link = ((y_down, YD), (y_up, YU))[way]
        slots = [POS[(left if way == 0 else 8 - left) % 8] for left in range(steps, 0, -1)]
        src, needs = pbuf.at[slots[0], :, part(q)], [parts[slots[0] // 2, q]]
        for t in range(steps):
            arrived = send(src, rbuf.at[q, way, t], peer, link, 32, needs, rank=0.01 * q)
            if t < steps - 1:
                def add(t=t, pos=slots[t + 1]):
                    rbuf[q, way, t] = (
                        rbuf[q, way, t].astype(F32) + pbuf[pos, :, q * QW : (q + 1) * QW].astype(F32)
                    ).astype(BF16)
                needs = [task(add, 0.06, [arrived, parts[slots[t + 1] // 2, q]], rank=0.0)]
                src = rbuf.at[q, way, t]
        return arrived, steps - 1

    chunk_in = []
    for q in range(Q):
        ends = [chain(q, way) for way in range(2)]

        def finish(q=q, ends=ends):
            cols = slice(q * QW, (q + 1) * QW)
            total = pbuf[POS[0], :, cols].astype(F32)
            for way in range(2):
                total += rbuf[q, way, ends[way][1]].astype(F32)
            feat[land, :, cols] = total.astype(BF16)

        finished = task(finish, 0.1, [parts[POS[0] // 2, q], *(arrived for arrived, _ in ends)], rank=0.0)
        own = feat.at[land, :, part(q)]
        far = send(own, own, z_far, (("z+", 2), ("z-", 2)), 32, [finished], hops=4)
        other = feat.at[land + 1 - 2 * zh, :, part(q)]
        chunk_in.append([finished, far])
        for piece, need in ((own, finished), (other, far)):
            chunk_in[q] += [
                send(piece, piece, x_peer[d], far_x(d), 32, [need], hops=1 + d % 2) for d in (2, 1, 3)
            ]

    step2 = []
    summed = []
    for h in range(H):
        cols = slice(h * HW, (h + 1) * HW)
        ds = pl.ds(h * HW, HW)

        def select(cols=cols):
            out = jnp.dot(pickb[...], feat[:, :, cols].reshape(512, HW), preferred_element_type=F32)
            obuf[:, :, cols] = out.reshape(8, 16, HW).astype(BF16)
            arr[0, :, cols] = out[:16].astype(BF16)

        chunks = [n for q in range(h * Q // H, (h + 1) * Q // H) for n in chunk_in[q]]
        selected = task(select, 0.3, [chosen, *chunks], rank=0.5)
        step1 = [
            send(obuf.at[d, :, ds], arr.at[d, :, ds], y_peer[d], far_y(d), 16, [selected], hops=min(d, 8 - d))
            for d in (4, 3, 5, 2, 6, 1, 7)
        ]

        def sum_up(h=h, cols=cols):
            sums = jnp.dot(matchb[...], arr[:, :, cols].reshape(128, HW), preferred_element_type=F32)
            mine[:, cols] = sums[:8]
            sums = sums.reshape(8, 8, HW)
            tsend[h] = jnp.concatenate([sums[:, :, : HW // 2], sums[:, :, HW // 2 :]], axis=1).astype(BF16)

        summed.append(task(sum_up, 0.3, [matched, selected, *step1], rank=0.6))
        step2 += [
            send(
                tsend.at[h, i], trecv.at[h, i], zc_peer[i],
                SC if i == 1 else ((("z+", 1), ("z-", 1))), 8, [summed[h]], hops=2,
            )
            for i in (7, 6, 5, 4, 3, 2, 1)
        ]

    def distances(b):
        def work():
            rows = feat[2 * b : 2 * b + 2].reshape(128, FW)
            wide = rows.astype(F32)
            feat_sq = jnp.sum(wide * wide, axis=1, keepdims=True)
            cross = lax.dot_general(rows, cbuf[...], (((1,), (1,)), ((), ())), preferred_element_type=F32)
            dist_ref[b * 128 : (b + 1) * 128, :] = (feat_sq + centq[...] - 2.0 * cross) * (1.0 / FW)
        return task(work, 0.5, [got_c, *squared, *(n for chunk in chunk_in for n in chunk)], rank=10.0)

    for b in range(4):
        distances(b)

    def means():
        counts = csend[0]
        for i in range(1, 8):
            counts += crecv[i]
        scale = 1.0 / jnp.maximum(counts[:, :1], 1.0)
        for h in range(H):
            total = jnp.sum(trecv[h, 1:].astype(F32), axis=0)
            total = mine[:, h * HW : (h + 1) * HW] + jnp.concatenate([total[:8], total[8:]], axis=1)
            newc_ref[:, h * HW : (h + 1) * HW] = total * scale

    task(means, 0.2, [*summed, *step2, *counts_in], rank=0.7)

    emit(nodes, loads)
    for copy in copies:
        copy.wait_send()


def local(embeddings, landmarks, factor, centroids, assignment):
    vmem = pl.BlockSpec(memory_space=pltpu.VMEM)
    anywhere = pl.BlockSpec(memory_space=pl.ANY)
    return pl.pallas_call(
        kernel,
        out_shape=(
            jax.ShapeDtypeStruct((512, 512), F32),
            jax.ShapeDtypeStruct((8, FW), F32),
        ),
        in_specs=[anywhere] * 5,
        out_specs=(vmem, vmem),
        scratch_shapes=[
            pltpu.VMEM((8, 64, EW), BF16),
            pltpu.VMEM((4, 2, 8, 16, EW), BF16),
            pltpu.VMEM((4, 2, 8, 16, FW), BF16),
            pltpu.VMEM((512, FW), BF16),
            pltpu.VMEM((512, 1024), BF16),
            pltpu.VMEM((8, 64, FW), BF16),
            pltpu.VMEM((Q, 2, 4, 64, QW), BF16),
            pltpu.VMEM((8, 64, FW), BF16),
            pltpu.VMEM((8, 1, 512), jnp.int32),
            pltpu.VMEM((8, 16, FW), BF16),
            pltpu.VMEM((8, 16, FW), BF16),
            pltpu.VMEM((H, 8, 16, HW // 2), BF16),
            pltpu.VMEM((H, 8, 16, HW // 2), BF16),
            pltpu.VMEM((8, 8, 128), F32),
            pltpu.VMEM((8, 8, 128), F32),
            pltpu.VMEM((512, 1), F32),
            pltpu.VMEM((4, 1, 256), F32),
            pltpu.VMEM((1, 512), F32),
            pltpu.VMEM((128, 512), BF16),
            pltpu.VMEM((64, 128), BF16),
            pltpu.VMEM((8, FW), F32),
            pltpu.SemaphoreType.DMA((N_SEM,)),
            pltpu.SemaphoreType.DMA((N_SEM,)),
            pltpu.SemaphoreType.DMA((5,)),
        ],
        compiler_params=pltpu.CompilerParams(
            collective_id=0, has_side_effects=True, vmem_limit_bytes=56 << 20
        ),
        name="nystrom",
    )(embeddings, landmarks, factor, centroids, assignment.reshape(1, 512))


def solution(mesh):
    return jax.shard_map(
        local,
        mesh=mesh,
        in_specs=(
            P(("dp", "land"), None),
            P(("land", "dp"), None),
            P(("land", "dp"), None),
            P("land", None),
            P("dp"),
        ),
        out_specs=(P("dp", "land"), P(("land", "dp"), None)),
        check_vma=False,
    )
```

```python
import jax
import jax.numpy as jnp
from jax import lax
from jax.experimental import pallas as pl
from jax.experimental.pallas import tpu as pltpu
from jax.sharding import PartitionSpec as P

EPSILON = 1e-06
SHARPNESS = 6.0
MESH = pl.DeviceIdType.MESH
BF16 = jnp.bfloat16
F32 = jnp.float32

NX, NZ, NY = 4, 8, 8
EW = 1280
FW = 1024
Q = 4
QW = FW // Q
H = 2
HW = FW // H
N_SEM = 330

POS = {4: 0, 5: 1, 3: 2, 6: 3, 2: 4, 7: 5, 1: 6, 0: 7}

PER_KB = 0.02
PER_KB_SIBLING = 0.002
HOP = 3.6
FURTHER = 0.95
EP = 4
FH = 2
LXU = (4,)
STEP = 0.025


class Node:
    def __init__(self, needs, work=None, cost=0.0, rank=0.0, copy=None, links=(), hops=1, kb=0.0):
        self.needs, self.work, self.cost, self.rank = needs, work, cost, rank
        self.copy, self.links, self.hops, self.kb = copy, links, hops, kb


def emit(nodes, flying):
    clock, free, done, sent = 0.0, {}, set(), []
    flying = [(node.kb / 200, k, node) for k, node in enumerate(flying)]
    waiting = list(nodes)
    count = len(flying)
    while waiting or flying:
        ready = [n for n in waiting if all(id(d) in done for d in n.needs)]
        sends = [n for n in ready if n.copy is not None]
        if sends:
            node = min(sends, key=lambda n: n.rank)
            node.copy.start()
            end = clock
            for link, hops in node.links:
                rate = PER_KB_SIBLING if link == "c" else PER_KB
                free[link] = max(clock, free.get(link, 0.0)) + node.kb * rate * hops
                end = max(end, free[link])
            flying.append((end + HOP + FURTHER * (node.hops - 1), count, node))
            sent.append((end + HOP, node))
            count += 1
            clock += STEP
            waiting.remove(node)
            continue
        tasks = [n for n in ready if n.copy is None]
        soonest = min(flying) if flying else None
        if soonest and (soonest[0] <= clock or not tasks):
            while sent and clock + 0.3 < soonest[0] and sent[0][0] + 1.0 < clock:
                sent.pop(0)[1].copy.wait_send()
                clock += 0.02
            flying.remove(soonest)
            (soonest[2].copy.wait_recv if soonest[2].links else soonest[2].copy.wait)()
            clock = max(clock, soonest[0]) + STEP
            done.add(id(soonest[2]))
            continue
        node = min(tasks, key=lambda n: n.rank)
        node.work()
        clock += node.cost
        done.add(id(node))
        waiting.remove(node)
    for _, node in sent:
        node.copy.wait_send()


def across(column):
    n = column.shape[0]
    spread = jnp.broadcast_to(column, (n, n))
    eye = lax.broadcasted_iota(jnp.int32, (n, n), 0) == lax.broadcasted_iota(jnp.int32, (n, n), 1)
    return jnp.sum(jnp.where(eye, spread, 0.0), axis=0, keepdims=True)


def kernel(
    e_ref, l_ref, f_ref, c_ref, a_ref,
    dist_ref, newc_ref,
    ebuf, lbuf, fbuf, cbuf, kbuf, pbuf, rbuf, feat, abuf, obuf, arr, tsend, trecv, csend, crecv,
    rowc, markc, centq, pickb, matchb, mine, ss, rs, ls,
):
    land = lax.axis_index("land")
    dp = lax.axis_index("dp")
    x, zh = land // 2, land % 2
    zl, y, c = dp // 16, (dp // 2) % 8, dp % 2
    z = zh * 4 + zl

    def device(dx=0, dz=0, dy=0, dc=0):
        xx, zz, yy, cc = (x + dx) % NX, (z + dz) % NZ, (y + dy) % NY, (c + dc) % 2
        return (xx * 2 + zz // 4, (zz % 4) * 16 + yy * 2 + cc)

    def near(rz, rc):
        return (land, ((zl + rz) % 4) * 16 + y * 2 + (c + rc) % 2)

    y_up, y_down = device(dy=1), device(dy=7)
    x_up, x_down = device(dx=1), device(dx=3)
    z_up, z_down = device(dz=1), device(dz=7)
    z_far = device(dz=4)
    sibling = device(dc=1)
    y_peer = {d: device(dy=d) for d in range(1, 8)}
    x_peer = {d: device(dx=d) for d in range(1, 4)}
    zc_peer = {i: near(i // 2, i % 2) for i in range(1, 8)}

    loads = []
    for src, dst in (
        (l_ref, lbuf.at[0, 0, 0]), (f_ref, fbuf.at[0, 0, 0]), (e_ref, ebuf.at[POS[0]]),
        (a_ref, abuf.at[0]), (c_ref, cbuf),
    ):
        copy = pltpu.make_async_copy(src, dst, ls.at[len(loads)])
        copy.start()
        loads.append(Node([], copy=copy, kb=src.size / 512))
    got_l, got_f, got_e, got_a, got_c = loads

    barrier = pltpu.get_barrier_semaphore()
    z_skip = {d: device(dz=d) for d in (2, 6)}
    peers = [
        z_far, *(y_peer[d] for d in (4, 3, 5, 2, 6)), *(zc_peer[i] for i in range(7, 0, -1)),
        *z_skip.values(), x_peer[2], z_up, z_down, y_up, y_down, x_up, x_down,
    ]
    for peer in peers:
        pl.semaphore_signal(barrier, inc=1, device_id=peer, device_id_type=MESH)
    pl.semaphore_wait(barrier, len(peers))

    nodes = []
    copies = []

    def task(work, cost, needs, rank=0.0):
        nodes.append(Node(needs, work=work, cost=cost, rank=rank))
        return nodes[-1]

    def send(src, dst, peer, links, kb, needs, hops=1, rank=0.0):
        k = len(copies)
        copies.append(
            pltpu.make_async_remote_copy(
                src_ref=src, dst_ref=dst, send_sem=ss.at[k], recv_sem=rs.at[k],
                device_id=peer, device_id_type=MESH,
            )
        )
        nodes.append(Node(needs, copy=copies[k], links=links, kb=kb, hops=hops, rank=rank))
        return nodes[-1]

    YU, YD, XU, XD, ZU, ZD, SC = [((name, 1),) for name in ("y+", "y-", "x+", "x-", "z+", "z-", "c")]

    def far_y(d):
        return (("y+", d),) if d < 4 else (("y-", 8 - d),) if d > 4 else (("y+", 2), ("y-", 2))

    def far_x(d):
        return {1: XU, 3: XD, 2: (("x+", 1), ("x-", 1))}[d]

    fcols = [pl.ds(h * FW // FH, FW // FH) for h in range(FH)]
    fkb = 32 // FH
    fz = {}

    def send_fx(h):
        own = fbuf.at[0, 0, 0, :, fcols[h]]
        fz[0, 0, h] = [got_f]
        for dx in (2, 1, 3):
            fz[dx, 0, h] = [
                send(own, fbuf.at[dx, 0, 0, :, fcols[h]], x_peer[dx], far_x(dx), fkb, [got_f], hops=2 - dx % 2, rank=0.1 * h)
            ]

    for h in range(FH):
        send_fx(h)

    lz = {0: [got_l]}
    own = lbuf.at[0, 0, 0]
    first, second = pl.ds(0, EW // 2), pl.ds(EW // 2, EW // 2)
    lz[2] = [send(own, lbuf.at[0, 0, 2], z_skip[2], (("z+", 2),), 40, [got_l], hops=2)]
    lz[6] = [send(own, lbuf.at[0, 0, 6], z_skip[6], (("z-", 2),), 40, [got_l], hops=2)]
    lz[1] = [send(own, lbuf.at[0, 0, 1], z_up, ZU, 40, [got_l])]
    lz[7] = [send(own, lbuf.at[0, 0, 7], z_down, ZD, 40, [got_l])]
    lz[4] = [
        send(lbuf.at[0, 0, 2, :, first], lbuf.at[0, 0, 4, :, first], z_skip[2], (("z+", 2),), 20, lz[2], hops=2),
        send(lbuf.at[0, 0, 6, :, second], lbuf.at[0, 0, 4, :, second], z_skip[6], (("z-", 2),), 20, lz[6], hops=2),
    ]
    lz[3] = [send(lbuf.at[0, 0, 2], lbuf.at[0, 0, 3], z_up, ZU, 40, lz[2])]
    lz[5] = [send(lbuf.at[0, 0, 6], lbuf.at[0, 0, 5], z_down, ZD, 40, lz[6])]

    half = [pl.ds(p * 64 // EP, 64 // EP) for p in range(EP)]
    e = {(0, p): [got_e] for p in range(EP)}
    for k in range(1, 5):
        for p in range(EP):
            up, down = (k - 1, p), ((9 - k) % 8, p)
            if k < 4 or p < EP // 2:
                e[k, p] = [send(ebuf.at[POS[up[0]], half[p]], ebuf.at[POS[k], half[p]], y_up, YU, 160 // EP, e[up])]
            if k < 4 or p >= EP // 2:
                e[8 - k, p] = [send(ebuf.at[POS[down[0]], half[p]], ebuf.at[POS[8 - k], half[p]], y_down, YD, 160 // EP, e[down])]

    lx = {}
    for dz in (0, 1, 7, 2, 6, 3, 5, 4):
        lx[0, dz] = lz[dz]
        lx[1, dz] = [send(lbuf.at[0, 0, dz], lbuf.at[1, 0, dz], x_up, XU, 40, lz[dz])]
        lx[3, dz] = [send(lbuf.at[0, 0, dz], lbuf.at[3, 0, dz], x_down, XD, 40, lz[dz])]
    for dz in (0, 1, 7, 2, 6, 3, 5, 4):
        if dz in LXU:
            lx[2, dz] = [send(lbuf.at[0, 0, dz], lbuf.at[2, 0, dz], x_peer[2], far_x(2), 40, lz[dz], hops=2)]
        elif dz < 4:
            lx[2, dz] = [send(lbuf.at[1, 0, dz], lbuf.at[2, 0, dz], x_up, XU, 40, lx[1, dz])]
        else:
            lx[2, dz] = [send(lbuf.at[3, 0, dz], lbuf.at[2, 0, dz], x_down, XD, 40, lx[3, dz])]

    def fpiece(dx, dz, h):
        return fbuf.at[dx, 0, dz, :, fcols[h]]

    for h in range(FH):
        rank = 0.1 + 0.1 * h
        for k in range(1, 5):
            for dx in (0, 1, 3, 2):
                up, down = (dx, k - 1, h), (dx, (9 - k) % 8, h)
                if k < 4 or dx < 2:
                    fz[dx, k, h] = [send(fpiece(*up), fpiece(dx, k, h), z_up, ZU, fkb, fz[up], rank=rank)]
                if k < 4 or dx >= 2:
                    fz[dx, 8 - k, h] = [send(fpiece(*down), fpiece(dx, 8 - k, h), z_down, ZD, fkb, fz[down], rank=rank)]

    lsib = {}
    for dx in range(4):
        lsib[dx] = [
            send(
                lbuf.at[dx, 0, pl.ds(4 * p, 4)], lbuf.at[dx, 1, pl.ds(4 * p, 4)], sibling, SC, 160,
                [n for dz in range(4 * p, 4 * p + 4) for n in lx[dx, dz]],
            )
            for p in range(2)
        ]
    fsib = {
        (k, h): send(
            fbuf.at[:, 0, k, :, fcols[h]], fbuf.at[:, 1, k, :, fcols[h]], sibling, SC, 4 * fkb,
            [n for dx in range(4) for n in fz[dx, k, h]],
        )
        for h in range(FH) for k in range(8)
    }

    def targets(a):
        to = (a >> 3) & 63
        ry, rz, rc = ((to >> 1) - y) & 7, ((to >> 4) - zl) & 3, (to - c) & 1
        return (a >> 9) == land, ry, rz * 2 + rc

    def picks(at, at_row):
        row = lax.broadcasted_iota(jnp.int32, at.shape, 1).astype(F32)
        here = at == at_row
        first = jnp.min(jnp.where(here, row, 1e4), axis=1, keepdims=True)
        last = jnp.max(jnp.where(here, row, -1.0), axis=1, keepdims=True)
        one = jnp.where(here & (row == first), 1.0, 0.0)
        two = jnp.where(here & (row == last) & (last != first), 1.0, 0.0)
        return one, two

    def choose():
        inside, ry, rzc = targets(abuf[0])
        at = jnp.broadcast_to(jnp.where(inside, ry * 8 + rzc, -1), (64, 512))
        one, two = picks(at, lax.broadcasted_iota(jnp.int32, (64, 512), 0))
        both = jnp.concatenate([one.reshape(8, 8, 512), two.reshape(8, 8, 512)], axis=1)
        pickb[...] = both.reshape(128, 512).astype(BF16)

    chosen = task(choose, 1.0, [got_a], rank=1.0)

    ids_in = [send(abuf.at[0], abuf.at[d], y_peer[d], far_y(d), 2, [got_a], rank=0.05) for d in range(1, 8)]

    def matching():
        a = abuf[...]
        inside, ry, rzc = targets(a)
        at = jnp.broadcast_to(jnp.where(inside & (ry == 0), rzc, -1), (8, 8, 512)).reshape(64, 512)
        number = jnp.broadcast_to((a & 7).astype(F32) + 1.0, (8, 8, 512)).reshape(64, 512)
        ids = [
            jnp.sum(which * number, axis=1, keepdims=True).reshape(8, 8, 1)
            for which in picks(at, lax.broadcasted_iota(jnp.int32, (64, 512), 0) & 7)
        ]
        ids = across(jnp.concatenate(ids, axis=1).reshape(128, 1)) - 1.0
        row = lax.broadcasted_iota(jnp.int32, (64, 128), 0)
        column = lax.broadcasted_iota(jnp.int32, (64, 128), 1)
        match = ((row >> 3) == (column & 7)) & ((row & 7).astype(F32) == jnp.broadcast_to(ids, (64, 128)))
        match = jnp.where(match, 1.0, 0.0)
        csend[...] = jnp.broadcast_to(jnp.sum(match, axis=1, keepdims=True), (64, 128)).reshape(8, 8, 128)
        matchb[...] = match.astype(BF16)

    matched = task(matching, 1.2, [got_a, *ids_in], rank=8.0)
    counts_in = [send(csend.at[i], crecv.at[i], zc_peer[i], SC, 4, [matched], rank=0.2) for i in range(1, 8)]

    def square_centroids(k):
        def work():
            rows = cbuf[k * 128 : (k + 1) * 128, :].astype(F32)
            centq[:, k * 128 : (k + 1) * 128] = across(jnp.sum(rows * rows, axis=1, keepdims=True))
        return task(work, 0.4, [got_c], rank=9.0)

    squared = [square_centroids(k) for k in range(4)]

    places = {pos: j for j, pos in POS.items()}

    def e_group(g):
        return [n for j in (places[2 * g], places[2 * g + 1]) for p in range(EP) for n in e[j, p]]

    def l_group(dx):
        return lsib[dx] + [n for dz in range(8) for n in lx[dx, dz]]

    def row_coef(g):
        def work():
            rows = ebuf[2 * g : 2 * g + 2].reshape(128, EW).astype(F32)
            mean = jnp.sum(rows * rows, axis=1, keepdims=True) * (1.0 / EW)
            rowc[g * 128 : (g + 1) * 128, :] = lax.rsqrt(mean + EPSILON) * (SHARPNESS / EW)
        return task(work, 0.3, e_group(g), rank=2.0)

    def mark_coef(dx):
        def work():
            marks = lbuf[dx].reshape(256, EW).astype(F32)
            mean = jnp.sum(marks * marks, axis=1, keepdims=True) * (1.0 / EW)
            scale = lax.rsqrt(mean + EPSILON)
            markc[dx] = jnp.concatenate([across(scale[:128]), across(scale[128:])], axis=1)
        return task(work, 0.5, l_group(dx), rank=2.0)

    row_done = [row_coef(g) for g in range(4)]
    mark_done = [mark_coef(dx) for dx in range(4)]

    def similar(g, dx):
        def work():
            dots = lax.dot_general(
                ebuf[2 * g : 2 * g + 2].reshape(128, EW), lbuf[dx].reshape(256, EW),
                (((1,), (1,)), ((), ())), preferred_element_type=F32,
            )
            rows = slice(g * 128, (g + 1) * 128)
            value = jnp.exp(dots * rowc[rows, :] * markc[dx] - SHARPNESS)
            kbuf[rows, dx * 256 : (dx + 1) * 256] = value.astype(BF16)
        return task(work, 0.18, [row_done[g], mark_done[dx]], rank=3.0 + 0.1 * g)

    tiles = {(g, dx): similar(g, dx) for g in range(4) for dx in range(4)}

    factor_in = [
        [n for key, n in fsib.items() if key[-1] == h] + [n for key, pieces in fz.items() if key[-1] == h for n in pieces]
        for h in range(FH)
    ]

    def partial(g, q):
        def work():
            cols = slice(q * QW, (q + 1) * QW)
            value = jnp.dot(
                kbuf[g * 128 : (g + 1) * 128, :], fbuf[:, :, :, :, cols].reshape(1024, QW),
                preferred_element_type=F32,
            )
            pbuf[2 * g : 2 * g + 2, :, cols] = value.reshape(2, 64, QW).astype(BF16)
        return task(work, 0.1, [*factor_in[q * FH // Q], *(tiles[g, dx] for dx in range(4))], rank=4.0 + g + 0.01 * q)

    parts = {(g, q): partial(g, q) for g in range(4) for q in range(Q)}

    def part(q):
        return pl.ds(q * QW, QW)

    def chain(q, way):
        steps = 4 if (q + way) % 2 == 0 else 3
        peer, link = ((y_down, YD), (y_up, YU))[way]
        slots = [POS[(left if way == 0 else 8 - left) % 8] for left in range(steps, 0, -1)]
        src, needs = pbuf.at[slots[0], :, part(q)], [parts[slots[0] // 2, q]]
        for t in range(steps):
            arrived = send(src, rbuf.at[q, way, t], peer, link, 32, needs, rank=0.01 * q)
            if t < steps - 1:
                def add(t=t, pos=slots[t + 1]):
                    rbuf[q, way, t] = (
                        rbuf[q, way, t].astype(F32) + pbuf[pos, :, q * QW : (q + 1) * QW].astype(F32)
                    ).astype(BF16)
                needs = [task(add, 0.06, [arrived, parts[slots[t + 1] // 2, q]], rank=0.0)]
                src = rbuf.at[q, way, t]
        return arrived, steps - 1

    chunk_in = []
    for q in range(Q):
        ends = [chain(q, way) for way in range(2)]

        def finish(q=q, ends=ends):
            cols = slice(q * QW, (q + 1) * QW)
            total = pbuf[POS[0], :, cols].astype(F32)
            for way in range(2):
                total += rbuf[q, way, ends[way][1]].astype(F32)
            feat[land, :, cols] = total.astype(BF16)

        finished = task(finish, 0.1, [parts[POS[0] // 2, q], *(arrived for arrived, _ in ends)], rank=0.0)
        own = feat.at[land, :, part(q)]
        far = send(own, own, z_far, (("z+", 2), ("z-", 2)), 32, [finished], hops=4)
        other = feat.at[land + 1 - 2 * zh, :, part(q)]
        chunk_in.append([finished, far])
        for piece, need in ((own, finished), (other, far)):
            chunk_in[q] += [
                send(piece, piece, x_peer[d], far_x(d), 32, [need], hops=2 - d % 2) for d in (2, 1, 3)
            ]

    step2 = []
    summed = []
    for h in range(H):
        cols = slice(h * HW, (h + 1) * HW)
        ds = pl.ds(h * HW, HW)

        def select(cols=cols):
            out = jnp.dot(pickb[...], feat[:, :, cols].reshape(512, HW), preferred_element_type=F32)
            obuf[:, :, cols] = out.reshape(8, 16, HW).astype(BF16)
            arr[0, :, cols] = out[:16].astype(BF16)

        chunks = [n for q in range(h * Q // H, (h + 1) * Q // H) for n in chunk_in[q]]
        selected = task(select, 0.3, [chosen, *chunks], rank=0.5)
        step1 = [
            send(obuf.at[d, :, ds], arr.at[d, :, ds], y_peer[d], far_y(d), 16, [selected], hops=min(d, 8 - d))
            for d in (4, 3, 5, 2, 6, 1, 7)
        ]

        def sum_up(h=h, cols=cols):
            sums = jnp.dot(matchb[...], arr[:, :, cols].reshape(128, HW), preferred_element_type=F32)
            mine[:, cols] = sums[:8]
            sums = sums.reshape(8, 8, HW)
            tsend[h] = jnp.concatenate([sums[:, :, : HW // 2], sums[:, :, HW // 2 :]], axis=1).astype(BF16)

        summed.append(task(sum_up, 0.3, [matched, selected, *step1], rank=0.6))
        step2 += [
            send(
                tsend.at[h, i], trecv.at[h, i], zc_peer[i],
                SC if i == 1 else ((("z+", 1), ("z-", 1))), 8, [summed[h]], hops=2,
            )
            for i in (7, 6, 5, 4, 3, 2, 1)
        ]

    def distances(b):
        def work():
            rows = feat[2 * b : 2 * b + 2].reshape(128, FW)
            wide = rows.astype(F32)
            feat_sq = jnp.sum(wide * wide, axis=1, keepdims=True)
            cross = lax.dot_general(rows, cbuf[...], (((1,), (1,)), ((), ())), preferred_element_type=F32)
            dist_ref[b * 128 : (b + 1) * 128, :] = (feat_sq + centq[...] - 2.0 * cross) * (1.0 / FW)
        return task(work, 0.5, [got_c, *squared, *(n for chunk in chunk_in for n in chunk)], rank=10.0)

    for b in range(4):
        distances(b)

    def means():
        counts = csend[0]
        for i in range(1, 8):
            counts += crecv[i]
        scale = 1.0 / jnp.maximum(counts[:, :1], 1.0)
        for h in range(H):
            total = jnp.sum(trecv[h, 1:].astype(F32), axis=0)
            total = mine[:, h * HW : (h + 1) * HW] + jnp.concatenate([total[:8], total[8:]], axis=1)
            newc_ref[:, h * HW : (h + 1) * HW] = total * scale

    task(means, 0.2, [*summed, *step2, *counts_in], rank=0.7)

    emit(nodes, loads)


def local(embeddings, landmarks, factor, centroids, assignment):
    vmem = pl.BlockSpec(memory_space=pltpu.VMEM)
    anywhere = pl.BlockSpec(memory_space=pl.ANY)
    return pl.pallas_call(
        kernel,
        out_shape=(
            jax.ShapeDtypeStruct((512, 512), F32),
            jax.ShapeDtypeStruct((8, FW), F32),
        ),
        in_specs=[anywhere] * 5,
        out_specs=(vmem, vmem),
        scratch_shapes=[
            pltpu.VMEM((8, 64, EW), BF16),
            pltpu.VMEM((4, 2, 8, 16, EW), BF16),
            pltpu.VMEM((4, 2, 8, 16, FW), BF16),
            pltpu.VMEM((512, FW), BF16),
            pltpu.VMEM((512, 1024), BF16),
            pltpu.VMEM((8, 64, FW), BF16),
            pltpu.VMEM((Q, 2, 4, 64, QW), BF16),
            pltpu.VMEM((8, 64, FW), BF16),
            pltpu.VMEM((8, 1, 512), jnp.int32),
            pltpu.VMEM((8, 16, FW), BF16),
            pltpu.VMEM((8, 16, FW), BF16),
            pltpu.VMEM((H, 8, 16, HW // 2), BF16),
            pltpu.VMEM((H, 8, 16, HW // 2), BF16),
            pltpu.VMEM((8, 8, 128), F32),
            pltpu.VMEM((8, 8, 128), F32),
            pltpu.VMEM((512, 1), F32),
            pltpu.VMEM((4, 1, 256), F32),
            pltpu.VMEM((1, 512), F32),
            pltpu.VMEM((128, 512), BF16),
            pltpu.VMEM((64, 128), BF16),
            pltpu.VMEM((8, FW), F32),
            pltpu.SemaphoreType.DMA((N_SEM,)),
            pltpu.SemaphoreType.DMA((N_SEM,)),
            pltpu.SemaphoreType.DMA((5,)),
        ],
        compiler_params=pltpu.CompilerParams(
            collective_id=0, has_side_effects=True, vmem_limit_bytes=56 << 20
        ),
        name="nystrom",
    )(embeddings, landmarks, factor, centroids, assignment.reshape(1, 512))


def solution(mesh):
    return jax.shard_map(
        local,
        mesh=mesh,
        in_specs=(
            P(("dp", "land"), None),
            P(("land", "dp"), None),
            P(("land", "dp"), None),
            P("land", None),
            P("dp"),
        ),
        out_specs=(P("dp", "land"), P(("land", "dp"), None)),
        check_vma=False,
    )
```
